32 devices in a mesh: ctx: 8 (over y, x, core), grp: 4 (over z).
Axes of the slice: x: 2, y: 2, z: 4, core: 2. Of those that a mesh axis runs over, the one named last changes fastest.
Arguments:
- queries: bfloat16 [1024, 4096], P('ctx', 'grp'), may hold values from -96 to 96
- key_value_pair: bfloat16 [1024, 2, 512], P('ctx', None, 'grp'), may hold values from -4 to 4
- attention_upstream: bfloat16 [1024, 4096], P('ctx', 'grp'), may hold values from -6 to 6
- ssm_input: bfloat16 [1024, 4096], P('ctx', 'grp'), may hold values from -6 to 6
- write_vec: bfloat16 [1024, 256], P('ctx'), may hold values from -0.375 to 0.375
- read_vec: bfloat16 [1024, 256], P('ctx'), may hold values from -0.375 to 0.375
- log_decay: float32 [1024, 64], P('ctx', 'grp'), may hold values from -1 to 0, as said below
- ssm_upstream: bfloat16 [1024, 4096], P('ctx', 'grp'), may hold values from -0.59765625 to 0.59765625
Outputs:
- attention_out: bfloat16 [1024, 4096], P('ctx', 'grp')
- queries_grad: bfloat16 [1024, 4096], P('ctx', 'grp')
- keyvalue_grad: bfloat16 [1024, 2, 512], P('ctx', None, 'grp')
- ssm_out: bfloat16 [1024, 4096], P('ctx', 'grp')
- input_grad: bfloat16 [1024, 4096], P('ctx', 'grp')
- write_grad: bfloat16 [1024, 256], P('ctx')
- read_grad: bfloat16 [1024, 256], P('ctx')
The draws below stay inside these ranges and needn't reach their ends.
Inputs may be any that keep to these rules, and one draw needn't show every extreme that they name: `log_decay`: every entry is below zero.
All inputs are finite; a program needn't handle non-finite values.
Results may differ from the reference program's by a relative error of at most 0.04.
Values may be sent and summed in bfloat16 or wider, within the bound.
A program may use at most 384 MiB of HBM per device.

```python
import jax
import jax.numpy as jnp
from jax import lax

HEAD_WIDTH = 128
QUERY_HEADS = 32
KEY_VALUE_HEADS = 4
HS = 64
P_SIZE = 64
N = 256
SPAN = 128
TOK_DEV = 128
SEQUENCE_TOKENS = 1024
KBLOCK = 512


def attention_base(key):
    key_value_pair = jnp.clip(jax.random.normal(jax.random.fold_in(key, 11), (SEQUENCE_TOKENS, 2, KEY_VALUE_HEADS, HEAD_WIDTH), jnp.float32), -4.0, 4.0)
    queries = jnp.clip(jax.random.normal(jax.random.fold_in(key, 12), (SEQUENCE_TOKENS, QUERY_HEADS, HEAD_WIDTH), jnp.float32), -4.0, 4.0)
    token_position = lax.iota(jnp.int32, SEQUENCE_TOKENS)
    half_keys = jnp.repeat(jnp.roll(key_value_pair[:, 0], SEQUENCE_TOKENS // 2, axis=0), QUERY_HEADS // KEY_VALUE_HEADS, axis=1)
    far_pick = (token_position % 16 == 3) & (token_position >= SEQUENCE_TOKENS // 2)
    queries = jnp.where(far_pick[:, None, None], 2.0 * half_keys, queries)
    return (queries, key_value_pair)


def draw_queries(key, part):
    queries = attention_base(key)[0]
    return queries.reshape(SEQUENCE_TOKENS, QUERY_HEADS * HEAD_WIDTH).astype(jnp.bfloat16)


def draw_key_value_pair(key, part):
    key_value_pair = attention_base(key)[1]
    return key_value_pair.reshape(SEQUENCE_TOKENS, 2, KEY_VALUE_HEADS * HEAD_WIDTH).astype(jnp.bfloat16)


def draw_log_decay(key, part):
    fast_share = 0.5
    fast = jax.random.uniform(jax.random.fold_in(key, 21), (HS,), jnp.float32) < fast_share
    slow_rate = jax.random.uniform(jax.random.fold_in(key, 22), (HS,), jnp.float32, 0.1, 0.8) / SEQUENCE_TOKENS
    fast_rate = jax.random.uniform(jax.random.fold_in(key, 23), (HS,), jnp.float32, 1.0 / 50.0, 1.0 / 30.0)
    rate = jnp.where(fast, fast_rate, slow_rate)
    token_factor = jnp.exp(jax.random.uniform(jax.random.fold_in(key, 24), (SEQUENCE_TOKENS, HS), jnp.float32, -0.6931, 0.6931))
    block_factor = jnp.exp(jax.random.uniform(jax.random.fold_in(key, 25), (SEQUENCE_TOKENS // TOK_DEV, HS), jnp.float32, -0.6931, 0.6931))
    block_factor = jnp.repeat(block_factor, TOK_DEV, axis=0)
    transfer_rounds = jax.random.randint(jax.random.fold_in(key, 26), (3,), 0, SEQUENCE_TOKENS)
    token_position = lax.iota(jnp.int32, SEQUENCE_TOKENS)
    match_flag = jnp.any(transfer_rounds[:, None] == token_position[None, :], axis=0)
    keep = jax.random.uniform(jax.random.fold_in(key, 27), (SEQUENCE_TOKENS,), jnp.float32, 0.6, 0.8)
    drop = jnp.where(match_flag, jnp.log(keep), 0.0)
    return (-rate[None, :] * token_factor * block_factor + drop[:, None]).astype(jnp.float32)


def block_levels(own_key, extent, shards, low, top_value):
    gain, own = 1.0, jax.random.fold_in(own_key, 6)
    for axis_at, parts in shards:
        heights = jnp.exp(jax.random.uniform(jax.random.fold_in(own, axis_at), (parts,), jnp.float32, low / len(shards), top_value / len(shards)))
        gain = gain * jnp.repeat(heights, extent[axis_at] // parts).reshape([-1 if axis == axis_at else 1 for axis in range(len(extent))])
    return gain


def gaussian(stream_key, extent, spread, bound, pieces=(), held_as=jnp.bfloat16):
    drawn = jax.random.normal(stream_key, extent, jnp.float32) * spread
    if len(pieces) > 0:
        drawn = block_levels(stream_key, extent, pieces, -0.22, 0.18) * drawn
    return jnp.clip(drawn, min=-bound, max=bound).astype(held_as)


def setup_inputs(seed: int = 0) -> dict:
    streams_of = jax.random.split(jax.random.key(seed), 9)
    queries = draw_queries(jax.random.fold_in(streams_of[8], 71), 0)
    key_value_pair = draw_key_value_pair(jax.random.fold_in(streams_of[8], 71), 0)
    attention_upstream = gaussian(streams_of[2], (SEQUENCE_TOKENS, QUERY_HEADS * HEAD_WIDTH), 1.0, 6.0, ((0, 8), (1, 4)))
    ssm_input = gaussian(streams_of[3], (SEQUENCE_TOKENS, HS * P_SIZE), 1.0, 6.0, ((0, 8), (1, 4)))
    write_vec = gaussian(streams_of[4], (SEQUENCE_TOKENS, N), (N ** -0.5), 0.375, ((0, 8),))
    read_vec = gaussian(streams_of[5], (SEQUENCE_TOKENS, N), (N ** -0.5), 0.375, ((0, 8),))
    log_decay = draw_log_decay(jax.random.fold_in(streams_of[8], 71), 0)
    ssm_upstream = gaussian(streams_of[7], (SEQUENCE_TOKENS, HS * P_SIZE), 0.1, 0.59765625, ((0, 8), (1, 4)))
    return dict(queries=queries, key_value_pair=key_value_pair, attention_upstream=attention_upstream, ssm_input=ssm_input, write_vec=write_vec, read_vec=read_vec, log_decay=log_decay, ssm_upstream=ssm_upstream)


HIGH = lax.Precision.HIGHEST


def attention_reference(queries, key_value_pair, attention_upstream):
    head_group = QUERY_HEADS // KEY_VALUE_HEADS
    scale = 1.0 / (HEAD_WIDTH ** 0.5)
    query_f = queries.reshape(SEQUENCE_TOKENS, QUERY_HEADS, HEAD_WIDTH).astype(jnp.float32)
    key_float = jnp.repeat(key_value_pair[:, 0].reshape(SEQUENCE_TOKENS, KEY_VALUE_HEADS, HEAD_WIDTH), head_group, axis=1).astype(jnp.float32)
    value_float = jnp.repeat(key_value_pair[:, 1].reshape(SEQUENCE_TOKENS, KEY_VALUE_HEADS, HEAD_WIDTH), head_group, axis=1).astype(jnp.float32)
    upstream = attention_upstream.reshape(SEQUENCE_TOKENS, QUERY_HEADS, HEAD_WIDTH).astype(jnp.float32)
    key_gradient = jnp.zeros((SEQUENCE_TOKENS, QUERY_HEADS, HEAD_WIDTH), jnp.float32)
    value_gradient = jnp.zeros((SEQUENCE_TOKENS, QUERY_HEADS, HEAD_WIDTH), jnp.float32)
    outputs = []
    qgrads = []
    for index in range(SEQUENCE_TOKENS // KBLOCK):
        first = index * KBLOCK
        final = first + KBLOCK
        qblock = query_f[first:final]
        ublock = upstream[first:final]
        kblock = key_float[:final]
        vblock = value_float[:final]
        scores = jnp.einsum("qhd,khd->hqk", qblock, kblock, precision=HIGH) * scale
        key_pos = jnp.arange(final, dtype=jnp.int32)
        query_pos = first + jnp.arange(KBLOCK, dtype=jnp.int32)
        valid = key_pos[None, :] <= query_pos[:, None]
        scores = jnp.where(valid[None], scores, -jnp.inf)
        log_total = jax.nn.logsumexp(scores, axis=-1)
        exact = jnp.exp(scores - log_total[..., None])
        probs = lax.optimization_barrier(exact.astype(jnp.bfloat16)).astype(jnp.float32)
        output = jnp.einsum("hqk,khd->qhd", probs, vblock, precision=HIGH).astype(jnp.bfloat16)
        row_dots = jnp.sum(ublock * output.astype(jnp.float32), axis=-1)
        probs_grad = jnp.einsum("qhd,khd->hqk", ublock, vblock, precision=HIGH)
        scores_grad = (exact * (probs_grad - jnp.transpose(row_dots)[..., None]) * scale)
        scores_grad = lax.optimization_barrier(scores_grad.astype(jnp.bfloat16)).astype(jnp.float32)
        qgrad = jnp.einsum("hqk,khd->qhd", scores_grad, kblock, precision=HIGH).astype(jnp.bfloat16)
        key_gradient = key_gradient.at[:final].add(jnp.einsum("hqk,qhd->khd", scores_grad, qblock, precision=HIGH))
        value_gradient = value_gradient.at[:final].add(jnp.einsum("hqk,qhd->khd", probs, ublock, precision=HIGH))
        outputs.append(output.reshape(KBLOCK, QUERY_HEADS * HEAD_WIDTH))
        qgrads.append(qgrad.reshape(KBLOCK, QUERY_HEADS * HEAD_WIDTH))
    key_total = key_gradient.reshape(SEQUENCE_TOKENS, KEY_VALUE_HEADS, head_group, HEAD_WIDTH).sum(axis=2).reshape(SEQUENCE_TOKENS, KEY_VALUE_HEADS * HEAD_WIDTH)
    value_total = value_gradient.reshape(SEQUENCE_TOKENS, KEY_VALUE_HEADS, head_group, HEAD_WIDTH).sum(axis=2).reshape(SEQUENCE_TOKENS, KEY_VALUE_HEADS * HEAD_WIDTH)
    pair = jnp.stack((key_total, value_total), axis=1).astype(jnp.bfloat16)
    return jnp.concatenate(outputs, axis=0), jnp.concatenate(qgrads, axis=0), pair


def block_terms(inputs, writes, reads, decay_log):
    cum_decay = jnp.cumsum(decay_log, axis=1)
    by_head = jnp.transpose(cum_decay, (0, 2, 1))
    length = cum_decay.shape[1]
    lower = lax.iota(jnp.int32, length)[:, None] >= lax.iota(jnp.int32, length)[None, :]
    gaps = by_head[:, :, :, None] - by_head[:, :, None, :]
    decay = jnp.exp(jnp.where(lower, gaps, -jnp.inf))
    gram = jnp.einsum("ctn,csn->cts", reads, writes, precision=HIGH)
    ssm_weights = decay * gram[:, None]
    growth = jnp.exp(cum_decay[:, -1, :])
    tails = jnp.exp(cum_decay[:, -1:, :] - cum_decay)
    heads_in = jnp.exp(cum_decay)
    updates = jnp.einsum("csjp,csn->cjpn", tails[..., None] * inputs, writes, precision=HIGH)
    return decay, ssm_weights, growth, tails, heads_in, updates


def block_outputs(inputs, reads, ssm_weights, heads_in, states):
    local = jnp.einsum("cjts,csjp->ctjp", ssm_weights, inputs, precision=HIGH)
    carried = jnp.einsum("cjpn,ctn->ctjp", states, reads, precision=HIGH) * heads_in[..., None]
    return local + carried


def adjoint_terms(upstream, reads, heads_in):
    return jnp.einsum("ctjp,ctn->cjpn", heads_in[..., None] * upstream, reads, precision=HIGH)


def block_grads(inputs, writes, reads, upstream, decay, ssm_weights, tails, heads_in, states, adjoints):
    input_grad = jnp.einsum("cjts,ctjp->csjp", ssm_weights, upstream, precision=HIGH)
    input_grad = input_grad + tails[..., None] * jnp.einsum("cjpn,csn->csjp", adjoints, writes, precision=HIGH)
    dots = jnp.einsum("ctjp,csjp->cjts", upstream, inputs, precision=HIGH)
    mixing = jnp.sum(decay * dots, axis=1)
    read_grad = jnp.einsum("cts,csn->ctn", mixing, writes, precision=HIGH)
    read_grad = read_grad + jnp.einsum("cjpn,ctjp->ctn", states, heads_in[..., None] * upstream, precision=HIGH)
    write_grad = jnp.einsum("cts,ctn->csn", mixing, reads, precision=HIGH)
    write_grad = write_grad + jnp.einsum("cjpn,csjp->csn", adjoints, tails[..., None] * inputs, precision=HIGH)
    return input_grad, read_grad, write_grad


def carry_forward(start, growth, updates):
    def advance(state, item):
        return item[0][:, None, None] * state + item[1], state
    return lax.scan(advance, start, (growth, updates))[1]


def carry_backward(start, growth, terms):
    def retreat(adjoint, item):
        return item[0][:, None, None] * adjoint + item[1], adjoint
    return lax.scan(retreat, start, (growth, terms), reverse=True)[1]


def ssm_reference(ssm_input, write_vec, read_vec, log_decay, ssm_upstream):
    blocks = SEQUENCE_TOKENS // SPAN
    inputs = ssm_input.astype(jnp.float32).reshape(blocks, SPAN, HS, P_SIZE)
    writes = write_vec.astype(jnp.float32).reshape(blocks, SPAN, N)
    reads = read_vec.astype(jnp.float32).reshape(blocks, SPAN, N)
    decay_log = log_decay.reshape(blocks, SPAN, HS)
    upstream = ssm_upstream.astype(jnp.float32).reshape(blocks, SPAN, HS, P_SIZE)
    decay, ssm_weights, growth, tails, heads_in, updates = block_terms(inputs, writes, reads, decay_log)
    zeros = jnp.zeros((HS, P_SIZE, N), jnp.float32)
    states = carry_forward(zeros, growth, updates)
    ssm_out = block_outputs(inputs, reads, ssm_weights, heads_in, states).reshape(SEQUENCE_TOKENS, HS * P_SIZE).astype(jnp.bfloat16)
    terms = adjoint_terms(upstream, reads, heads_in)
    adjoints = carry_backward(zeros, growth, terms)
    input_grad, read_grad, write_grad = block_grads(inputs, writes, reads, upstream, decay, ssm_weights, tails, heads_in, states, adjoints)
    return (ssm_out, input_grad.reshape(SEQUENCE_TOKENS, HS * P_SIZE).astype(jnp.bfloat16),
            write_grad.reshape(SEQUENCE_TOKENS, N).astype(jnp.bfloat16), read_grad.reshape(SEQUENCE_TOKENS, N).astype(jnp.bfloat16))


def reference(queries, key_value_pair, attention_upstream, ssm_input, write_vec, read_vec, log_decay, ssm_upstream):
    attention_out, queries_grad, keyvalue_grad = attention_reference(queries, key_value_pair, attention_upstream)
    ssm_out, input_grad, write_grad, read_grad = ssm_reference(ssm_input, write_vec, read_vec, log_decay, ssm_upstream)
    return (attention_out, queries_grad, keyvalue_grad, ssm_out, input_grad, write_grad, read_grad)
```

```python
import functools
import math

import jax
import jax.numpy as jnp
from jax import lax
from jax.experimental import pallas as pl
from jax.experimental.pallas import tpu as pltpu
from jax.sharding import PartitionSpec as P

HEAD_WIDTH = 128
MESH = pl.DeviceIdType.MESH
HIGH = lax.Precision.HIGHEST
BF16 = jnp.bfloat16
F32 = jnp.float32


def dot(a, b, ca, cb, precision=None):
    return lax.dot_general(
        a, b, (((ca,), (cb,)), ((), ())), preferred_element_type=F32, precision=precision
    )


def kernel(
    n,
    ng,
    q_ref,
    kv_ref,
    up_ref,
    x_ref,
    wr_ref,
    rd_ref,
    ld_ref,
    su_ref,
    out_ref,
    qg_ref,
    kvg_ref,
    so_ref,
    ig_ref,
    wg_ref,
    rg_ref,
    kv_all,
    tot_all,
    u_own,
    t_own,
    u_sib,
    t_sib,
    u_chip,
    t_chip,
    fw_buf,
    bw_buf,
    s_acc,
    a_acc,
    s_send,
    a_send,
    s_full,
    a_full,
    xs_buf,
    us_buf,
    tails_buf,
    heads_buf,
    rw_acc,
    rs_send,
    rs_buf,
    ag_buf,
    top_buf,
    norm_buf,
    dots_buf,
    outt_buf,
    dqt_buf,
    dkv_send,
    dkv_buf,
    dkv_own,
    kv_s,
    kv_r,
    tot_s,
    tot_r,
    sib_s,
    sib_r,
    fw_s,
    fw_r,
    bw_s,
    bw_r,
    dk_s,
    dk_r,
    rs_s,
    rs_r,
    ag_s,
    ag_r,
):
    rows = q_ref.shape[0]
    heads_q = q_ref.shape[1] // HEAD_WIDTH
    heads = ld_ref.shape[1]
    width = x_ref.shape[1] // heads
    flat = x_ref.shape[1]
    half = flat // 2
    half_heads = heads // 2
    scale = 1.0 / math.sqrt(HEAD_WIDTH)
    chips = n // 2
    me = lax.axis_index("ctx")
    grp = lax.axis_index("grp")
    core = lax.rem(me, 2)
    chip = me // 2
    sib = me + 1 - 2 * core
    part = rows // ng
    my_half = pl.multiple_of(core * half, half)
    sib_half = pl.multiple_of((1 - core) * half, half)
    my_rows = pl.multiple_of(me * rows, rows)

    barrier = pltpu.get_barrier_semaphore()

    def greet(d, _):
        @pl.when(d != me)
        def _():
            pl.semaphore_signal(barrier, inc=1, device_id={"ctx": d}, device_id_type=MESH)

        return 0

    def greet_grp(d, _):
        @pl.when(d != grp)
        def _():
            pl.semaphore_signal(barrier, inc=1, device_id={"grp": d}, device_id_type=MESH)

        return 0

    lax.fori_loop(0, n, greet, 0)
    lax.fori_loop(0, ng, greet_grp, 0)

    def kv_copy(src, dest):
        at = pl.multiple_of(src * rows, rows)
        return pltpu.make_async_remote_copy(
            src_ref=kv_ref,
            dst_ref=kv_all.at[pl.ds(at, rows)],
            send_sem=kv_s.at[dest],
            recv_sem=kv_r.at[src],
            device_id={"ctx": dest},
            device_id_type=MESH,
        )

    def tot_copy(src, dest):
        return pltpu.make_async_remote_copy(
            src_ref=tot_all.at[src],
            dst_ref=tot_all.at[src],
            send_sem=tot_s.at[dest],
            recv_sem=tot_r.at[src],
            device_id={"ctx": dest},
            device_id_type=MESH,
        )

    def sib_copy(src_ref, dst_ref, which):
        return pltpu.make_async_remote_copy(
            src_ref=src_ref,
            dst_ref=dst_ref,
            send_sem=sib_s.at[which],
            recv_sem=sib_r.at[which],
            device_id={"ctx": sib},
            device_id_type=MESH,
        )

    def chip_copy(src_ref, buf, ssem, rsem, src, dest):
        return pltpu.make_async_remote_copy(
            src_ref=src_ref,
            dst_ref=buf.at[src],
            send_sem=ssem.at[dest],
            recv_sem=rsem.at[src],
            device_id={"ctx": 2 * dest + core},
            device_id_type=MESH,
        )

    def dkv_copy(src, dest):
        at = pl.multiple_of(dest * rows, rows)
        return pltpu.make_async_remote_copy(
            src_ref=dkv_send.at[pl.ds(at, rows)],
            dst_ref=dkv_buf.at[src],
            send_sem=dk_s.at[dest],
            recv_sem=dk_r.at[src],
            device_id={"ctx": dest},
            device_id_type=MESH,
        )

    def rs_copy(src, dest):
        at = pl.multiple_of(dest * part, part)
        return pltpu.make_async_remote_copy(
            src_ref=rs_send.at[pl.ds(at, part)],
            dst_ref=rs_buf.at[src],
            send_sem=rs_s.at[dest],
            recv_sem=rs_r.at[src],
            device_id={"grp": dest},
            device_id_type=MESH,
        )

    def ag_copy(src, dest):
        at = pl.multiple_of(src * part, part)
        return pltpu.make_async_remote_copy(
            src_ref=ag_buf.at[pl.ds(at, part)],
            dst_ref=ag_buf.at[pl.ds(at, part)],
            send_sem=ag_s.at[dest],
            recv_sem=ag_r.at[src],
            device_id={"grp": dest},
            device_id_type=MESH,
        )

    def each(low, high, action):
        def body(d, _):
            action(d)
            return 0

        lax.fori_loop(low, high, body, 0)

    decay_log = ld_ref[...]
    row_id = lax.broadcasted_iota(jnp.int32, (rows, rows), 0)
    col_id = lax.broadcasted_iota(jnp.int32, (rows, rows), 1)
    lower = row_id >= col_id
    cum = dot(lower.astype(F32), decay_log, 1, 0, HIGH)
    cum_t = dot(decay_log, (row_id <= col_id).astype(F32), 0, 0, HIGH)
    last = cum[rows - 1 :, :]
    tot = dot(decay_log, jnp.ones((rows, tot_all.shape[2]), F32), 0, 0, HIGH)
    tot_all[me] = tot
    pick = (
        lax.broadcasted_iota(jnp.int32, (heads, flat), 1) // width
        == lax.broadcasted_iota(jnp.int32, (heads, flat), 0)
    ).astype(F32)
    tails = dot(jnp.exp(last - cum), pick, 1, 0, HIGH)
    heads_in = dot(jnp.exp(cum), pick, 1, 0, HIGH)
    tails_buf[...] = tails
    heads_buf[...] = heads_in
    xs_buf[...] = (tails * x_ref[...].astype(F32)).astype(BF16)
    us_buf[...] = (heads_in * su_ref[...].astype(F32)).astype(BF16)
    u_own[...] = dot(xs_buf[...], wr_ref[...], 0, 0).astype(BF16)
    t_own[...] = dot(us_buf[...], rd_ref[...], 0, 0).astype(BF16)

    pl.semaphore_wait(barrier, n - 1 + ng - 1)
    sib_u = sib_copy(u_own.at[pl.ds(sib_half, half)], u_sib, 0)
    sib_t = sib_copy(t_own.at[pl.ds(sib_half, half)], t_sib, 1)
    tot_copy(me, sib).start()
    sib_u.start()
    sib_t.start()

    def send_tot(d):
        @pl.when(d // 2 != chip)
        def _():
            tot_copy(me, d).start()

    each(0, n, send_tot)

    def send_kv(d):
        @pl.when(d != me)
        def _():
            kv_copy(me, d).start()

    each(2 * chip, n, send_kv)
    kv_all[pl.ds(my_rows, rows), :] = kv_ref[...]

    tot_copy(sib, sib).wait_recv()
    sib_u.wait_recv()
    sib_t.wait_recv()
    head_at = pl.multiple_of(core * half_heads, half_heads)
    first = core == 0

    def total_of(device):
        return tot_all[device, pl.ds(head_at, half_heads), :]

    grow_even = jnp.exp(total_of(2 * chip))
    grow_odd = jnp.exp(total_of(2 * chip + 1))

    def pair_of(own, other, h):
        mine = own[pl.ds(pl.multiple_of(my_half + h * width, width), width), :].astype(F32)
        theirs = other[pl.ds(h * width, width), :].astype(F32)
        return jnp.where(first, mine, theirs), jnp.where(first, theirs, mine)

    for h in range(half_heads):
        even, odd = pair_of(u_own, u_sib, h)
        u_chip[h * width : (h + 1) * width, :] = (
            grow_odd[h : h + 1, :] * even + odd
        ).astype(BF16)
        even, odd = pair_of(t_own, t_sib, h)
        t_chip[h * width : (h + 1) * width, :] = (
            even + grow_even[h : h + 1, :] * odd
        ).astype(BF16)

    each(chip + 1, chips, lambda d: chip_copy(u_chip, fw_buf, fw_s, fw_r, chip, d).start())
    each(0, chip, lambda d: chip_copy(t_chip, bw_buf, bw_s, bw_r, chip, d).start())

    gram = dot(rd_ref[...], wr_ref[...], 1, 1)
    gram2 = jnp.concatenate([gram, gram], axis=1)
    lane_low = lax.broadcasted_iota(jnp.int32, (rows, 2 * width), 1) < width
    mixing2 = jnp.zeros((rows, 2 * rows), F32)
    zero = jnp.zeros((rows, 2 * width), BF16)
    for p in range(heads // 2):
        cols = slice(2 * width * p, 2 * width * (p + 1))
        decays = []
        for h in (2 * p, 2 * p + 1):
            gap = cum[:, h : h + 1] - cum_t[h : h + 1, :]
            decays.append(jnp.exp(jnp.where(lower, gap, -jnp.inf)))
        decay = jnp.concatenate(decays, axis=1)
        weights = (decay * gram2).astype(BF16)
        x_pair = x_ref[:, cols]
        x_split = jnp.concatenate(
            [jnp.where(lane_low, x_pair, zero), jnp.where(lane_low, zero, x_pair)], axis=0
        )
        su_pair = su_ref[:, cols]
        mixing2 = mixing2 + decay * dot(su_pair, x_split, 1, 1)
        outt = dot(weights, x_split, 1, 0)
        so_ref[:, cols] = outt.astype(BF16)
        back = dot(weights, su_pair, 0, 0)
        ig_ref[:, cols] = jnp.where(lane_low, back[:rows], back[rows:]).astype(BF16)
    mixing = (mixing2[:, :rows] + mixing2[:, rows:]).astype(BF16)
    n_state = wr_ref.shape[1]
    rw_acc[:, :n_state] = dot(mixing, rd_ref[...], 0, 0)
    rw_acc[:, n_state:] = dot(mixing, wr_ref[...], 1, 0)

    block = 2 * rows
    key_id = lax.broadcasted_iota(jnp.int32, (block, rows), 0)
    query_id = lax.broadcasted_iota(jnp.int32, (block, rows), 1)

    top_buf[...] = jnp.full(top_buf.shape, -jnp.inf, F32)
    norm_buf[...] = jnp.zeros(norm_buf.shape, F32)
    outt_buf[...] = jnp.zeros(outt_buf.shape, F32)

    def forward(j):
        for d in (2 * j, 2 * j + 1):

            @pl.when(d != me)
            def _():
                kv_copy(d, sib).wait_recv()

        at = pl.multiple_of(j * block, block)
        keys = kv_all[pl.ds(at, block), :HEAD_WIDTH]
        values_t = kv_all[pl.ds(at, block), HEAD_WIDTH:].T
        valid = key_id + j * block <= query_id + me * rows
        for h in range(heads_q):
            q = q_ref[:, h * HEAD_WIDTH : (h + 1) * HEAD_WIDTH]
            scores = jnp.where(valid, dot(keys, q, 1, 1) * scale, -jnp.inf)
            top = top_buf[h : h + 1, :]
            new_top = jnp.maximum(top, jnp.max(scores, axis=0, keepdims=True))
            shrink = jnp.exp(top - new_top)
            probs = jnp.exp(scores - new_top)
            norm_buf[h : h + 1, :] = norm_buf[h : h + 1, :] * shrink + jnp.sum(
                probs, axis=0, keepdims=True
            )
            top_buf[h : h + 1, :] = new_top
            outt_buf[h] = outt_buf[h] * shrink + dot(values_t, probs.astype(BF16), 1, 0)

    each(0, chip + 1, forward)

    s_acc[...] = jnp.zeros(s_acc.shape, F32)
    a_acc[...] = jnp.zeros(a_acc.shape, F32)

    def wait_tot(d):
        @pl.when(d // 2 != chip)
        def _():
            tot_copy(d, sib).wait_recv()

    each(0, n, wait_tot)

    def fold(acc, buf, rsem, src_ref, k):
        chip_copy(src_ref, buf, rsem, rsem, k, chip).wait_recv()
        grow = jnp.exp(total_of(2 * k) + total_of(2 * k + 1))
        for h in range(half_heads):
            at = slice(h * width, (h + 1) * width)
            acc[at, :] = grow[h : h + 1, :] * acc[at, :] + buf[k, at, :].astype(F32)

    each(0, chip, lambda k: fold(s_acc, fw_buf, fw_r, u_chip, k))
    each(
        0,
        chips - 1 - chip,
        lambda i: fold(a_acc, bw_buf, bw_r, t_chip, chips - 1 - i),
    )
    for h in range(half_heads):
        at = slice(h * width, (h + 1) * width)
        mine_at = pl.ds(pl.multiple_of(my_half + h * width, width), width)
        even_u, _ = pair_of(u_own, u_sib, h)
        state_even = s_acc[at, :]
        state_odd = grow_even[h : h + 1, :] * state_even + even_u
        s_full[mine_at, :] = jnp.where(first, state_even, state_odd).astype(BF16)
        s_send[at, :] = jnp.where(first, state_odd, state_even).astype(BF16)
        _, odd_t = pair_of(t_own, t_sib, h)
        adj_odd = a_acc[at, :]
        adj_even = grow_odd[h : h + 1, :] * adj_odd + odd_t
        a_full[mine_at, :] = jnp.where(first, adj_even, adj_odd).astype(BF16)
        a_send[at, :] = jnp.where(first, adj_odd, adj_even).astype(BF16)
    back_s = sib_copy(s_send, s_full.at[pl.ds(my_half, half)], 2)
    back_a = sib_copy(a_send, a_full.at[pl.ds(my_half, half)], 3)
    back_s.start()
    back_a.start()

    for h in range(heads_q):
        cols = slice(h * HEAD_WIDTH, (h + 1) * HEAD_WIDTH)
        norm = norm_buf[h : h + 1, :]
        low = (outt_buf[h] / norm).astype(BF16).astype(F32)
        out = low.T
        out_ref[:, cols] = out.astype(BF16)
        up_t = up_ref[:, cols].astype(F32).T
        dots_buf[h : h + 1, :] = jnp.sum(up_t * low, axis=0, keepdims=True)
        top_buf[h : h + 1, :] = top_buf[h : h + 1, :] + jnp.log(norm)
    dqt_buf[...] = jnp.zeros(dqt_buf.shape, F32)

    sib_copy(s_send, s_full.at[pl.ds(sib_half, half)], 2).wait_recv()
    sib_copy(a_send, a_full.at[pl.ds(sib_half, half)], 3).wait_recv()
    rw_acc[:, n_state:] = rw_acc[:, n_state:] + dot(us_buf[...], s_full[...], 1, 0)
    rw_acc[:, :n_state] = rw_acc[:, :n_state] + dot(xs_buf[...], a_full[...], 1, 0)
    rs_send[...] = rw_acc[...].astype(BF16)

    def send_rs(d):
        @pl.when(d != grp)
        def _():
            rs_copy(grp, d).start()

    each(0, ng, send_rs)
    so_ref[...] = (
        so_ref[...].astype(F32) + heads_buf[...] * dot(rd_ref[...], s_full[...], 1, 1)
    ).astype(BF16)
    ig_ref[...] = (
        ig_ref[...].astype(F32) + tails_buf[...] * dot(wr_ref[...], a_full[...], 1, 1)
    ).astype(BF16)

    def backward(j):
        at = pl.multiple_of(j * block, block)
        keys = kv_all[pl.ds(at, block), :HEAD_WIDTH]
        values = kv_all[pl.ds(at, block), HEAD_WIDTH:]
        keys_t = keys.T
        valid = key_id + j * block <= query_id + me * rows
        key_acc = jnp.zeros((block, HEAD_WIDTH), F32)
        value_acc = jnp.zeros((block, HEAD_WIDTH), F32)
        for h in range(heads_q):
            cols = slice(h * HEAD_WIDTH, (h + 1) * HEAD_WIDTH)
            q = q_ref[:, cols]
            up = up_ref[:, cols]
            scores = jnp.where(valid, dot(keys, q, 1, 1) * scale, -jnp.inf)
            exact = jnp.exp(scores - top_buf[h : h + 1, :])
            probs_grad = dot(values, up, 1, 1)
            scores_grad = (exact * (probs_grad - dots_buf[h : h + 1, :]) * scale).astype(BF16)
            dqt_buf[h] = dqt_buf[h] + dot(keys_t, scores_grad, 1, 0)
            key_acc = key_acc + dot(scores_grad, q, 1, 0)
            value_acc = value_acc + dot(exact.astype(BF16), up, 1, 0)
        dkv_send[pl.ds(at, block), :HEAD_WIDTH] = key_acc.astype(BF16)
        dkv_send[pl.ds(at, block), HEAD_WIDTH:] = value_acc.astype(BF16)

        @pl.when(j == chip)
        def _():
            own = core == 0
            dkv_own[:, :HEAD_WIDTH] = jnp.where(own, key_acc[:rows], key_acc[rows:])
            dkv_own[:, HEAD_WIDTH:] = jnp.where(own, value_acc[:rows], value_acc[rows:])

        for d in (2 * j, 2 * j + 1):

            @pl.when(d < me)
            def _():
                dkv_copy(me, d).start()

    each(0, chip + 1, backward)

    total = rw_acc[pl.ds(pl.multiple_of(grp * part, part), part), :]
    rw_acc[pl.ds(0, part), :] = total

    def take_rs(d):
        @pl.when(d != grp)
        def _():
            rs_copy(d, d).wait_recv()
            rw_acc[pl.ds(0, part), :] = rw_acc[pl.ds(0, part), :] + rs_buf[d].astype(F32)

    each(0, ng, take_rs)
    ag_buf[pl.ds(pl.multiple_of(grp * part, part), part), :] = rw_acc[pl.ds(0, part), :].astype(
        BF16
    )

    def send_ag(d):
        @pl.when(d != grp)
        def _():
            ag_copy(grp, d).start()

    each(0, ng, send_ag)

    for h in range(heads_q):
        qg_ref[:, h * HEAD_WIDTH : (h + 1) * HEAD_WIDTH] = dqt_buf[h].T.astype(BF16)

    def take_dkv(d):
        dkv_copy(d, me).wait_recv()
        dkv_own[...] = dkv_own[...] + dkv_buf[d].astype(F32)

    each(me + 1, n, take_dkv)
    kvg_ref[...] = dkv_own[...].astype(BF16)

    def take_ag(d):
        @pl.when(d != grp)
        def _():
            ag_copy(d, d).wait_recv()

    each(0, ng, take_ag)
    wg_ref[...] = ag_buf[:, :n_state]
    rg_ref[...] = ag_buf[:, n_state:]

    def end_ctx(d):
        @pl.when(d != me)
        def _():
            tot_copy(me, d).wait_send()

            @pl.when(d >= 2 * chip)
            def _():
                kv_copy(me, d).wait_send()

            @pl.when(d < me)
            def _():
                dkv_copy(me, d).wait_send()

    each(0, n, end_ctx)
    sib_u.wait_send()
    sib_t.wait_send()
    back_s.wait_send()
    back_a.wait_send()
    each(chip + 1, chips, lambda d: chip_copy(u_chip, fw_buf, fw_s, fw_r, chip, d).wait_send())
    each(0, chip, lambda d: chip_copy(t_chip, bw_buf, bw_s, bw_r, chip, d).wait_send())

    def end_grp(d):
        @pl.when(d != grp)
        def _():
            rs_copy(grp, d).wait_send()
            ag_copy(grp, d).wait_send()

    each(0, ng, end_grp)


def on_device(
    queries,
    key_value_pair,
    attention_upstream,
    ssm_input,
    write_vec,
    read_vec,
    log_decay,
    ssm_upstream,
):
    n = lax.axis_size("ctx")
    ng = lax.axis_size("grp")
    rows, cols = queries.shape
    heads_q = cols // HEAD_WIDTH
    flat = ssm_input.shape[1]
    heads = log_decay.shape[1]
    n_state = write_vec.shape[1]
    chips = n // 2
    half = flat // 2
    pair = key_value_pair.reshape(rows, 2 * HEAD_WIDTH)
    vm = pltpu.VMEM
    dma = pltpu.SemaphoreType.DMA
    outs = pl.pallas_call(
        functools.partial(kernel, n, ng),
        out_shape=(
            jax.ShapeDtypeStruct((rows, cols), BF16),
            jax.ShapeDtypeStruct((rows, cols), BF16),
            jax.ShapeDtypeStruct((rows, 2 * HEAD_WIDTH), BF16),
            jax.ShapeDtypeStruct((rows, flat), BF16),
            jax.ShapeDtypeStruct((rows, flat), BF16),
            jax.ShapeDtypeStruct((rows, n_state), BF16),
            jax.ShapeDtypeStruct((rows, n_state), BF16),
        ),
        in_specs=[pl.BlockSpec(memory_space=pltpu.VMEM)] * 8,
        out_specs=[pl.BlockSpec(memory_space=pltpu.VMEM)] * 7,
        scratch_shapes=[
            vm((n * rows, 2 * HEAD_WIDTH), BF16),
            vm((n, heads, n_state), F32),
            vm((flat, n_state), BF16),
            vm((flat, n_state), BF16),
            vm((half, n_state), BF16),
            vm((half, n_state), BF16),
            vm((half, n_state), BF16),
            vm((half, n_state), BF16),
            vm((chips, half, n_state), BF16),
            vm((chips, half, n_state), BF16),
            vm((half, n_state), F32),
            vm((half, n_state), F32),
            vm((half, n_state), BF16),
            vm((half, n_state), BF16),
            vm((flat, n_state), BF16),
            vm((flat, n_state), BF16),
            vm((rows, flat), BF16),
            vm((rows, flat), BF16),
            vm((rows, flat), F32),
            vm((rows, flat), F32),
            vm((rows, 2 * n_state), F32),
            vm((rows, 2 * n_state), BF16),
            vm((ng, rows // ng, 2 * n_state), BF16),
            vm((rows, 2 * n_state), BF16),
            vm((heads_q, rows), F32),
            vm((heads_q, rows), F32),
            vm((heads_q, rows), F32),
            vm((heads_q, HEAD_WIDTH, rows), F32),
            vm((heads_q, HEAD_WIDTH, rows), F32),
            vm((n * rows, 2 * HEAD_WIDTH), BF16),
            vm((n, rows, 2 * HEAD_WIDTH), BF16),
            vm((rows, 2 * HEAD_WIDTH), F32),
            dma((n,)),
            dma((n,)),
            dma((n,)),
            dma((n,)),
            dma((4,)),
            dma((4,)),
            dma((chips,)),
            dma((chips,)),
            dma((chips,)),
            dma((chips,)),
            dma((n,)),
            dma((n,)),
            dma((ng,)),
            dma((ng,)),
            dma((ng,)),
            dma((ng,)),
        ],
        compiler_params=pltpu.CompilerParams(
            collective_id=0, has_side_effects=True, vmem_limit_bytes=56 * 1024 * 1024
        ),
    )(
        queries,
        pair,
        attention_upstream,
        ssm_input,
        write_vec,
        read_vec,
        log_decay,
        ssm_upstream,
    )
    out, qg, kvg, so, ig, wg, rg = outs
    return (out, qg, kvg.reshape(rows, 2, HEAD_WIDTH), so, ig, wg, rg)


def solution(mesh):
    return jax.shard_map(
        on_device,
        mesh=mesh,
        in_specs=(
            P("ctx", "grp"),
            P("ctx", None, "grp"),
            P("ctx", "grp"),
            P("ctx", "grp"),
            P("ctx", None),
            P("ctx", None),
            P("ctx", "grp"),
            P("ctx", "grp"),
        ),
        out_specs=(
            P("ctx", "grp"),
            P("ctx", "grp"),
            P("ctx", None, "grp"),
            P("ctx", "grp"),
            P("ctx", "grp"),
            P("ctx", None),
            P("ctx", None),
        ),
        check_vma=False,
    )
```

```python
import functools
import math

import jax
import jax.numpy as jnp
from jax import lax
from jax.experimental import pallas as pl
from jax.experimental.pallas import tpu as pltpu
from jax.sharding import PartitionSpec as P

HEAD_WIDTH = 128
MESH = pl.DeviceIdType.MESH
HIGH = lax.Precision.HIGHEST
BF16 = jnp.bfloat16
F32 = jnp.float32


def dot(a, b, ca, cb, precision=None):
    return lax.dot_general(
        a, b, (((ca,), (cb,)), ((), ())), preferred_element_type=F32, precision=precision
    )


def kernel(
    n,
    ng,
    q_ref,
    kv_ref,
    up_ref,
    x_ref,
    wr_ref,
    rd_ref,
    ld_ref,
    su_ref,
    out_ref,
    qg_ref,
    kvg_ref,
    so_ref,
    ig_ref,
    wg_ref,
    rg_ref,
    kv_all,
    tot_all,
    u_own,
    t_own,
    u_sib,
    t_sib,
    u_chip,
    t_chip,
    fw_buf,
    bw_buf,
    s_acc,
    a_acc,
    s_send,
    a_send,
    s_full,
    a_full,
    xs_buf,
    us_buf,
    tails_buf,
    heads_buf,
    rw_acc,
    rs_send,
    rs_buf,
    ag_buf,
    top_buf,
    norm_buf,
    dots_buf,
    outt_buf,
    dqt_buf,
    dkv_send,
    dkv_buf,
    dkv_own,
    kv_s,
    kv_r,
    tot_s,
    tot_r,
    sib_s,
    sib_r,
    fw_s,
    fw_r,
    bw_s,
    bw_r,
    dk_s,
    dk_r,
    rs_s,
    rs_r,
    ag_s,
    ag_r,
):
    rows = q_ref.shape[0]
    heads_q = q_ref.shape[1] // HEAD_WIDTH
    heads = ld_ref.shape[0]
    width = x_ref.shape[1] // heads
    flat = x_ref.shape[1]
    half = flat // 2
    half_heads = heads // 2
    scale = 1.0 / math.sqrt(HEAD_WIDTH)
    chips = n // 2
    me = lax.axis_index("ctx")
    grp = lax.axis_index("grp")
    core = lax.rem(me, 2)
    chip = me // 2
    sib = me + 1 - 2 * core
    part = rows // ng
    my_half = pl.multiple_of(core * half, half)
    sib_half = pl.multiple_of((1 - core) * half, half)
    my_rows = pl.multiple_of(me * rows, rows)

    barrier = pltpu.get_barrier_semaphore()

    def greet(d, _):
        @pl.when(d != me)
        def _():
            pl.semaphore_signal(barrier, inc=1, device_id={"ctx": d}, device_id_type=MESH)

        return 0

    def greet_grp(d, _):
        @pl.when(d != grp)
        def _():
            pl.semaphore_signal(barrier, inc=1, device_id={"grp": d}, device_id_type=MESH)

        return 0

    lax.fori_loop(0, n, greet, 0)
    lax.fori_loop(0, ng, greet_grp, 0)

    def kv_copy(src, dest):
        at = pl.multiple_of(src * rows, rows)
        return pltpu.make_async_remote_copy(
            src_ref=kv_all.at[pl.ds(at, rows)],
            dst_ref=kv_all.at[pl.ds(at, rows)],
            send_sem=kv_s.at[dest],
            recv_sem=kv_r.at[src],
            device_id={"ctx": dest},
            device_id_type=MESH,
        )

    def tot_copy(src, dest):
        return pltpu.make_async_remote_copy(
            src_ref=tot_all.at[src],
            dst_ref=tot_all.at[src],
            send_sem=tot_s.at[dest],
            recv_sem=tot_r.at[src],
            device_id={"ctx": dest},
            device_id_type=MESH,
        )

    def sib_copy(src_ref, dst_ref, which):
        return pltpu.make_async_remote_copy(
            src_ref=src_ref,
            dst_ref=dst_ref,
            send_sem=sib_s.at[which],
            recv_sem=sib_r.at[which],
            device_id={"ctx": sib},
            device_id_type=MESH,
        )

    def chip_copy(src_ref, buf, ssem, rsem, src, dest):
        return pltpu.make_async_remote_copy(
            src_ref=src_ref,
            dst_ref=buf.at[src],
            send_sem=ssem.at[dest],
            recv_sem=rsem.at[src],
            device_id={"ctx": 2 * dest + core},
            device_id_type=MESH,
        )

    def dkv_copy(src, dest):
        at = pl.multiple_of(dest * rows, rows)
        return pltpu.make_async_remote_copy(
            src_ref=dkv_send.at[pl.ds(at, rows)],
            dst_ref=dkv_buf.at[src],
            send_sem=dk_s.at[dest],
            recv_sem=dk_r.at[src],
            device_id={"ctx": dest},
            device_id_type=MESH,
        )

    def rs_copy(src, dest):
        at = pl.multiple_of(dest * part, part)
        return pltpu.make_async_remote_copy(
            src_ref=rs_send.at[pl.ds(at, part)],
            dst_ref=rs_buf.at[src],
            send_sem=rs_s.at[dest],
            recv_sem=rs_r.at[src],
            device_id={"grp": dest},
            device_id_type=MESH,
        )

    def ag_copy(src, dest):
        at = pl.multiple_of(src * part, part)
        return pltpu.make_async_remote_copy(
            src_ref=ag_buf.at[pl.ds(at, part)],
            dst_ref=ag_buf.at[pl.ds(at, part)],
            send_sem=ag_s.at[dest],
            recv_sem=ag_r.at[src],
            device_id={"grp": dest},
            device_id_type=MESH,
        )

    def each(low, high, action):
        def body(d, _):
            action(d)
            return 0

        lax.fori_loop(low, high, body, 0)

    decay_log = ld_ref[...]
    row_id = lax.broadcasted_iota(jnp.int32, (rows, rows), 0)
    col_id = lax.broadcasted_iota(jnp.int32, (rows, rows), 1)
    lower = row_id >= col_id
    cum = dot(lower.astype(F32), decay_log, 1, 1, HIGH)
    cum_t = dot(decay_log, (row_id <= col_id).astype(F32), 1, 0, HIGH)
    last = cum[rows - 1 :, :]
    tot_all[me] = jnp.broadcast_to(cum_t[:, rows - 1 :], tot_all.shape[1:])
    pick = (
        lax.broadcasted_iota(jnp.int32, (heads, flat), 1) // width
        == lax.broadcasted_iota(jnp.int32, (heads, flat), 0)
    ).astype(F32)
    tails = dot(jnp.exp(last - cum), pick, 1, 0, HIGH)
    heads_in = dot(jnp.exp(cum), pick, 1, 0, HIGH)
    tails_buf[...] = tails
    heads_buf[...] = heads_in
    xs_buf[...] = (tails * x_ref[...].astype(F32)).astype(BF16)
    us_buf[...] = (heads_in * su_ref[...].astype(F32)).astype(BF16)
    u_own[...] = dot(xs_buf[...], wr_ref[...], 0, 0).astype(BF16)
    t_own[...] = dot(us_buf[...], rd_ref[...], 0, 0).astype(BF16)

    kv_all[pl.ds(my_rows, rows), :HEAD_WIDTH] = kv_ref[:, 0, :]
    kv_all[pl.ds(my_rows, rows), HEAD_WIDTH:] = kv_ref[:, 1, :]

    pl.semaphore_wait(barrier, n - 1 + ng - 1)
    sib_u = sib_copy(u_own.at[pl.ds(sib_half, half)], u_sib, 0)
    sib_t = sib_copy(t_own.at[pl.ds(sib_half, half)], t_sib, 1)
    tot_copy(me, sib).start()
    sib_u.start()
    sib_t.start()

    def send_tot(d):
        @pl.when(d // 2 != chip)
        def _():
            tot_copy(me, d).start()

    each(0, n, send_tot)

    def send_kv(d):
        @pl.when(d != me)
        def _():
            kv_copy(me, d).start()

    each(2 * chip, n, send_kv)

    tot_copy(sib, sib).wait_recv()
    sib_u.wait_recv()
    sib_t.wait_recv()
    head_at = pl.multiple_of(core * half_heads, half_heads)
    first = core == 0

    def total_of(device):
        return tot_all[device, pl.ds(head_at, half_heads), :]

    grow_even = jnp.exp(total_of(2 * chip))
    grow_odd = jnp.exp(total_of(2 * chip + 1))

    def pair_of(own, other, h):
        mine = own[pl.ds(pl.multiple_of(my_half + h * width, width), width), :].astype(F32)
        theirs = other[pl.ds(h * width, width), :].astype(F32)
        return jnp.where(first, mine, theirs), jnp.where(first, theirs, mine)

    for h in range(half_heads):
        even, odd = pair_of(u_own, u_sib, h)
        u_chip[h * width : (h + 1) * width, :] = (
            grow_odd[h : h + 1, :] * even + odd
        ).astype(BF16)
        even, odd = pair_of(t_own, t_sib, h)
        t_chip[h * width : (h + 1) * width, :] = (
            even + grow_even[h : h + 1, :] * odd
        ).astype(BF16)

    each(chip + 1, chips, lambda d: chip_copy(u_chip, fw_buf, fw_s, fw_r, chip, d).start())
    each(0, chip, lambda d: chip_copy(t_chip, bw_buf, bw_s, bw_r, chip, d).start())

    gram = dot(rd_ref[...], wr_ref[...], 1, 1)
    gram2 = jnp.concatenate([gram, gram], axis=1)
    lane_low = lax.broadcasted_iota(jnp.int32, (rows, 2 * width), 1) < width
    mixing2 = jnp.zeros((rows, 2 * rows), F32)
    zero = jnp.zeros((rows, 2 * width), BF16)
    for p in range(heads // 2):
        cols = slice(2 * width * p, 2 * width * (p + 1))
        decays = []
        for h in (2 * p, 2 * p + 1):
            gap = cum[:, h : h + 1] - cum_t[h : h + 1, :]
            decays.append(jnp.exp(jnp.where(lower, gap, -jnp.inf)))
        decay = jnp.concatenate(decays, axis=1)
        weights = (decay * gram2).astype(BF16)
        x_pair = x_ref[:, cols]
        x_split = jnp.concatenate(
            [jnp.where(lane_low, x_pair, zero), jnp.where(lane_low, zero, x_pair)], axis=0
        )
        su_pair = su_ref[:, cols]
        mixing2 = mixing2 + decay * dot(su_pair, x_split, 1, 1)
        outt = dot(weights, x_split, 1, 0)
        so_ref[:, cols] = outt.astype(BF16)
        back = dot(weights, su_pair, 0, 0)
        ig_ref[:, cols] = jnp.where(lane_low, back[:rows], back[rows:]).astype(BF16)
    mixing = (mixing2[:, :rows] + mixing2[:, rows:]).astype(BF16)
    n_state = wr_ref.shape[1]
    rw_acc[:, :n_state] = dot(mixing, rd_ref[...], 0, 0)
    rw_acc[:, n_state:] = dot(mixing, wr_ref[...], 1, 0)

    block = 2 * rows
    key_id = lax.broadcasted_iota(jnp.int32, (block, rows), 0)
    query_id = lax.broadcasted_iota(jnp.int32, (block, rows), 1)

    top_buf[...] = jnp.full(top_buf.shape, -jnp.inf, F32)
    norm_buf[...] = jnp.zeros(norm_buf.shape, F32)
    outt_buf[...] = jnp.zeros(outt_buf.shape, F32)

    def forward(j):
        for d in (2 * j, 2 * j + 1):

            @pl.when(d != me)
            def _():
                kv_copy(d, sib).wait_recv()

        at = pl.multiple_of(j * block, block)
        keys = kv_all[pl.ds(at, block), :HEAD_WIDTH]
        values_t = kv_all[pl.ds(at, block), HEAD_WIDTH:].T
        valid = key_id + j * block <= query_id + me * rows
        for h in range(heads_q):
            q = q_ref[:, h * HEAD_WIDTH : (h + 1) * HEAD_WIDTH]
            scores = jnp.where(valid, dot(keys, q, 1, 1) * scale, -jnp.inf)
            top = top_buf[h : h + 1, :]
            new_top = jnp.maximum(top, jnp.max(scores, axis=0, keepdims=True))
            shrink = jnp.exp(top - new_top)
            probs = jnp.exp(scores - new_top)
            norm_buf[h : h + 1, :] = norm_buf[h : h + 1, :] * shrink + jnp.sum(
                probs, axis=0, keepdims=True
            )
            top_buf[h : h + 1, :] = new_top
            outt_buf[h] = outt_buf[h] * shrink + dot(values_t, probs.astype(BF16), 1, 0)

    each(0, chip + 1, forward)

    for h in range(heads_q):
        cols = slice(h * HEAD_WIDTH, (h + 1) * HEAD_WIDTH)
        norm = norm_buf[h : h + 1, :]
        low = (outt_buf[h] / norm).astype(BF16).astype(F32)
        out = low.T
        out_ref[:, cols] = out.astype(BF16)
        up_t = up_ref[:, cols].astype(F32).T
        dots_buf[h : h + 1, :] = jnp.sum(up_t * low, axis=0, keepdims=True)
        top_buf[h : h + 1, :] = top_buf[h : h + 1, :] + jnp.log(norm)
    dqt_buf[...] = jnp.zeros(dqt_buf.shape, F32)

    def backward(j):
        at = pl.multiple_of(j * block, block)
        keys = kv_all[pl.ds(at, block), :HEAD_WIDTH]
        values = kv_all[pl.ds(at, block), HEAD_WIDTH:]
        keys_t = keys.T
        valid = key_id + j * block <= query_id + me * rows
        key_acc = jnp.zeros((block, HEAD_WIDTH), F32)
        value_acc = jnp.zeros((block, HEAD_WIDTH), F32)
        for h in range(heads_q):
            cols = slice(h * HEAD_WIDTH, (h + 1) * HEAD_WIDTH)
            q = q_ref[:, cols]
            up = up_ref[:, cols]
            scores = jnp.where(valid, dot(keys, q, 1, 1) * scale, -jnp.inf)
            exact = jnp.exp(scores - top_buf[h : h + 1, :])
            probs_grad = dot(values, up, 1, 1)
            scores_grad = (exact * (probs_grad - dots_buf[h : h + 1, :]) * scale).astype(BF16)
            dqt_buf[h] = dqt_buf[h] + dot(keys_t, scores_grad, 1, 0)
            key_acc = key_acc + dot(scores_grad, q, 1, 0)
            value_acc = value_acc + dot(exact.astype(BF16), up, 1, 0)
        dkv_send[pl.ds(at, block), :HEAD_WIDTH] = key_acc.astype(BF16)
        dkv_send[pl.ds(at, block), HEAD_WIDTH:] = value_acc.astype(BF16)

        @pl.when(j == chip)
        def _():
            own = core == 0
            dkv_own[:, :HEAD_WIDTH] = jnp.where(own, key_acc[:rows], key_acc[rows:])
            dkv_own[:, HEAD_WIDTH:] = jnp.where(own, value_acc[:rows], value_acc[rows:])

        for d in (2 * j, 2 * j + 1):

            @pl.when(d < me)
            def _():
                dkv_copy(me, d).start()

    each(0, chip + 1, backward)

    s_acc[...] = jnp.zeros(s_acc.shape, F32)
    a_acc[...] = jnp.zeros(a_acc.shape, F32)

    def wait_tot(d):
        @pl.when(d // 2 != chip)
        def _():
            tot_copy(d, sib).wait_recv()

    each(0, n, wait_tot)

    def fold(acc, buf, rsem, src_ref, k):
        chip_copy(src_ref, buf, rsem, rsem, k, chip).wait_recv()
        grow = jnp.exp(total_of(2 * k) + total_of(2 * k + 1))
        for h in range(half_heads):
            at = slice(h * width, (h + 1) * width)
            acc[at, :] = grow[h : h + 1, :] * acc[at, :] + buf[k, at, :].astype(F32)

    each(0, chip, lambda k: fold(s_acc, fw_buf, fw_r, u_chip, k))
    each(
        0,
        chips - 1 - chip,
        lambda i: fold(a_acc, bw_buf, bw_r, t_chip, chips - 1 - i),
    )
    for h in range(half_heads):
        at = slice(h * width, (h + 1) * width)
        mine_at = pl.ds(pl.multiple_of(my_half + h * width, width), width)
        even_u, _ = pair_of(u_own, u_sib, h)
        state_even = s_acc[at, :]
        state_odd = grow_even[h : h + 1, :] * state_even + even_u
        s_full[mine_at, :] = jnp.where(first, state_even, state_odd).astype(BF16)
        s_send[at, :] = jnp.where(first, state_odd, state_even).astype(BF16)
        _, odd_t = pair_of(t_own, t_sib, h)
        adj_odd = a_acc[at, :]
        adj_even = grow_odd[h : h + 1, :] * adj_odd + odd_t
        a_full[mine_at, :] = jnp.where(first, adj_even, adj_odd).astype(BF16)
        a_send[at, :] = jnp.where(first, adj_odd, adj_even).astype(BF16)
    back_s = sib_copy(s_send, s_full.at[pl.ds(my_half, half)], 2)
    back_a = sib_copy(a_send, a_full.at[pl.ds(my_half, half)], 3)
    back_s.start()
    back_a.start()

    sib_copy(s_send, s_full.at[pl.ds(sib_half, half)], 2).wait_recv()
    sib_copy(a_send, a_full.at[pl.ds(sib_half, half)], 3).wait_recv()
    rw_acc[:, n_state:] = rw_acc[:, n_state:] + dot(us_buf[...], s_full[...], 1, 0)
    rw_acc[:, :n_state] = rw_acc[:, :n_state] + dot(xs_buf[...], a_full[...], 1, 0)
    rs_send[...] = rw_acc[...].astype(BF16)

    def send_rs(d):
        @pl.when(d != grp)
        def _():
            rs_copy(grp, d).start()

    each(0, ng, send_rs)
    so_ref[...] = (
        so_ref[...].astype(F32) + heads_buf[...] * dot(rd_ref[...], s_full[...], 1, 1)
    ).astype(BF16)
    ig_ref[...] = (
        ig_ref[...].astype(F32) + tails_buf[...] * dot(wr_ref[...], a_full[...], 1, 1)
    ).astype(BF16)

    total = rw_acc[pl.ds(pl.multiple_of(grp * part, part), part), :]
    rw_acc[pl.ds(0, part), :] = total

    def take_rs(d):
        @pl.when(d != grp)
        def _():
            rs_copy(d, d).wait_recv()
            rw_acc[pl.ds(0, part), :] = rw_acc[pl.ds(0, part), :] + rs_buf[d].astype(F32)

    each(0, ng, take_rs)
    ag_buf[pl.ds(pl.multiple_of(grp * part, part), part), :] = rw_acc[pl.ds(0, part), :].astype(
        BF16
    )

    def send_ag(d):
        @pl.when(d != grp)
        def _():
            ag_copy(grp, d).start()

    each(0, ng, send_ag)

    for h in range(heads_q):
        qg_ref[:, h * HEAD_WIDTH : (h + 1) * HEAD_WIDTH] = dqt_buf[h].T.astype(BF16)

    def take_dkv(d):
        dkv_copy(d, me).wait_recv()
        dkv_own[...] = dkv_own[...] + dkv_buf[d].astype(F32)

    each(me + 1, n, take_dkv)
    kvg_ref[...] = dkv_own[...].astype(BF16)

    def take_ag(d):
        @pl.when(d != grp)
        def _():
            ag_copy(d, d).wait_recv()

    each(0, ng, take_ag)
    wg_ref[...] = ag_buf[:, :n_state]
    rg_ref[...] = ag_buf[:, n_state:]

    def end_ctx(d):
        @pl.when(d != me)
        def _():
            tot_copy(me, d).wait_send()

            @pl.when(d >= 2 * chip)
            def _():
                kv_copy(me, d).wait_send()

            @pl.when(d < me)
            def _():
                dkv_copy(me, d).wait_send()

    each(0, n, end_ctx)
    sib_u.wait_send()
    sib_t.wait_send()
    back_s.wait_send()
    back_a.wait_send()
    each(chip + 1, chips, lambda d: chip_copy(u_chip, fw_buf, fw_s, fw_r, chip, d).wait_send())
    each(0, chip, lambda d: chip_copy(t_chip, bw_buf, bw_s, bw_r, chip, d).wait_send())

    def end_grp(d):
        @pl.when(d != grp)
        def _():
            rs_copy(grp, d).wait_send()
            ag_copy(grp, d).wait_send()

    each(0, ng, end_grp)


def store(*refs):
    for index in range(7):
        source, target = refs[index], refs[7 + index]
        if index == 2:
            target[:, 0, :] = source[:, :HEAD_WIDTH]
            target[:, 1, :] = source[:, HEAD_WIDTH:]
        else:
            target[...] = source[...]


def on_device(
    queries,
    key_value_pair,
    attention_upstream,
    ssm_input,
    write_vec,
    read_vec,
    log_decay,
    ssm_upstream,
):
    n = lax.axis_size("ctx")
    ng = lax.axis_size("grp")
    rows, cols = queries.shape
    heads_q = cols // HEAD_WIDTH
    flat = ssm_input.shape[1]
    heads = log_decay.shape[1]
    n_state = write_vec.shape[1]
    chips = n // 2
    half = flat // 2
    vm = pltpu.VMEM
    dma = pltpu.SemaphoreType.DMA
    outs = pl.pallas_call(
        functools.partial(kernel, n, ng),
        out_shape=(
            jax.ShapeDtypeStruct((rows, cols), BF16),
            jax.ShapeDtypeStruct((rows, cols), BF16),
            jax.ShapeDtypeStruct((rows, 2 * HEAD_WIDTH), BF16),
            jax.ShapeDtypeStruct((rows, flat), BF16),
            jax.ShapeDtypeStruct((rows, flat), BF16),
            jax.ShapeDtypeStruct((rows, n_state), BF16),
            jax.ShapeDtypeStruct((rows, n_state), BF16),
        ),
        in_specs=[pl.BlockSpec(memory_space=pltpu.VMEM)] * 8,
        out_specs=[pl.BlockSpec(memory_space=pltpu.VMEM)] * 7,
        scratch_shapes=[
            vm((n * rows, 2 * HEAD_WIDTH), BF16),
            vm((n, heads, n_state), F32),
            vm((flat, n_state), BF16),
            vm((flat, n_state), BF16),
            vm((half, n_state), BF16),
            vm((half, n_state), BF16),
            vm((half, n_state), BF16),
            vm((half, n_state), BF16),
            vm((chips, half, n_state), BF16),
            vm((chips, half, n_state), BF16),
            vm((half, n_state), F32),
            vm((half, n_state), F32),
            vm((half, n_state), BF16),
            vm((half, n_state), BF16),
            vm((flat, n_state), BF16),
            vm((flat, n_state), BF16),
            vm((rows, flat), BF16),
            vm((rows, flat), BF16),
            vm((rows, flat), F32),
            vm((rows, flat), F32),
            vm((rows, 2 * n_state), F32),
            vm((rows, 2 * n_state), BF16),
            vm((ng, rows // ng, 2 * n_state), BF16),
            vm((rows, 2 * n_state), BF16),
            vm((heads_q, rows), F32),
            vm((heads_q, rows), F32),
            vm((heads_q, rows), F32),
            vm((heads_q, HEAD_WIDTH, rows), F32),
            vm((heads_q, HEAD_WIDTH, rows), F32),
            vm((n * rows, 2 * HEAD_WIDTH), BF16),
            vm((n, rows, 2 * HEAD_WIDTH), BF16),
            vm((rows, 2 * HEAD_WIDTH), F32),
            dma((n,)),
            dma((n,)),
            dma((n,)),
            dma((n,)),
            dma((4,)),
            dma((4,)),
            dma((chips,)),
            dma((chips,)),
            dma((chips,)),
            dma((chips,)),
            dma((n,)),
            dma((n,)),
            dma((ng,)),
            dma((ng,)),
            dma((ng,)),
            dma((ng,)),
        ],
        compiler_params=pltpu.CompilerParams(
            collective_id=0, has_side_effects=True, vmem_limit_bytes=56 * 1024 * 1024
        ),
    )(
        queries,
        key_value_pair,
        attention_upstream,
        ssm_input,
        write_vec,
        read_vec,
        log_decay.T,
        ssm_upstream,
    )
    return pl.pallas_call(
        store,
        out_shape=(
            jax.ShapeDtypeStruct((rows, cols), BF16),
            jax.ShapeDtypeStruct((rows, cols), BF16),
            jax.ShapeDtypeStruct((rows, 2, HEAD_WIDTH), BF16),
            jax.ShapeDtypeStruct((rows, flat), BF16),
            jax.ShapeDtypeStruct((rows, flat), BF16),
            jax.ShapeDtypeStruct((rows, n_state), BF16),
            jax.ShapeDtypeStruct((rows, n_state), BF16),
        ),
        in_specs=[pl.BlockSpec(memory_space=pltpu.VMEM)] * 7,
        out_specs=[pl.BlockSpec(memory_space=pltpu.VMEM)] * 7,
    )(*outs)


def solution(mesh):
    return jax.shard_map(
        on_device,
        mesh=mesh,
        in_specs=(
            P("ctx", "grp"),
            P("ctx", None, "grp"),
            P("ctx", "grp"),
            P("ctx", "grp"),
            P("ctx", None),
            P("ctx", None),
            P("ctx", "grp"),
            P("ctx", "grp"),
        ),
        out_specs=(
            P("ctx", "grp"),
            P("ctx", "grp"),
            P("ctx", None, "grp"),
            P("ctx", "grp"),
            P("ctx", "grp"),
            P("ctx", None),
            P("ctx", None),
        ),
        check_vma=False,
    )
```

```python
import functools
import math

import jax
import jax.numpy as jnp
from jax import lax
from jax.experimental import pallas as pl
from jax.experimental.pallas import tpu as pltpu
from jax.sharding import PartitionSpec as P

HEAD_WIDTH = 128
MESH = pl.DeviceIdType.MESH
HIGH = lax.Precision.HIGHEST
PIECES = 2
BF16 = jnp.bfloat16
F32 = jnp.float32


def dot(a, b, ca, cb, precision=None):
    return lax.dot_general(
        a, b, (((ca,), (cb,)), ((), ())), preferred_element_type=F32, precision=precision
    )


def kernel(
    n,
    ng,
    q_ref,
    kv_ref,
    up_ref,
    x_ref,
    wr_ref,
    rd_ref,
    ld_ref,
    su_ref,
    out_ref,
    qg_ref,
    kvg_ref,
    so_ref,
    ig_ref,
    wg_ref,
    rg_ref,
    kv_all,
    tot_all,
    u_own,
    t_own,
    u_sib,
    t_sib,
    u_chip,
    t_chip,
    fw_buf,
    bw_buf,
    s_acc,
    a_acc,
    s_send,
    a_send,
    s_full,
    a_full,
    xs_buf,
    us_buf,
    tails_buf,
    heads_buf,
    rw_acc,
    rs_send,
    rs_buf,
    ag_buf,
    top_buf,
    norm_buf,
    dots_buf,
    outt_buf,
    dqt_buf,
    dkv_send,
    dkv_buf,
    dkv_own,
    kv_s,
    kv_r,
    tot_s,
    tot_r,
    sib_s,
    sib_r,
    fw_s,
    fw_r,
    bw_s,
    bw_r,
    dk_s,
    dk_r,
    rs_s,
    rs_r,
    ag_s,
    ag_r,
):
    rows = q_ref.shape[0]
    heads_q = q_ref.shape[1] // HEAD_WIDTH
    heads = ld_ref.shape[0]
    width = x_ref.shape[1] // heads
    flat = x_ref.shape[1]
    half = flat // 2
    half_heads = heads // 2
    scale = 1.0 / math.sqrt(HEAD_WIDTH)
    chips = n // 2
    me = lax.axis_index("ctx")
    grp = lax.axis_index("grp")
    core = lax.rem(me, 2)
    chip = me // 2
    sib = me + 1 - 2 * core
    part = rows // ng
    heads_piece = half_heads // PIECES
    piece = heads_piece * width
    my_half = pl.multiple_of(core * half, half)
    sib_half = pl.multiple_of((1 - core) * half, half)
    my_rows = pl.multiple_of(me * rows, rows)

    barrier = pltpu.get_barrier_semaphore()

    def greet(d, _):
        @pl.when(d != me)
        def _():
            pl.semaphore_signal(barrier, inc=1, device_id={"ctx": d}, device_id_type=MESH)

        return 0

    def greet_grp(d, _):
        @pl.when(d != grp)
        def _():
            pl.semaphore_signal(barrier, inc=1, device_id={"grp": d}, device_id_type=MESH)

        return 0

    lax.fori_loop(0, n, greet, 0)
    lax.fori_loop(0, ng, greet_grp, 0)

    def kv_copy(src, dest, send=None):
        at = pl.multiple_of(src * rows, rows)
        return pltpu.make_async_remote_copy(
            src_ref=kv_all.at[pl.ds(at, rows)],
            dst_ref=kv_all.at[pl.ds(at, rows)],
            send_sem=kv_s.at[dest if send is None else send],
            recv_sem=kv_r.at[src],
            device_id={"ctx": dest},
            device_id_type=MESH,
        )

    def tot_copy(src, dest):
        return pltpu.make_async_remote_copy(
            src_ref=tot_all.at[src],
            dst_ref=tot_all.at[src],
            send_sem=tot_s.at[dest],
            recv_sem=tot_r.at[src],
            device_id={"ctx": dest},
            device_id_type=MESH,
        )

    def sib_copy(src_ref, dst_ref, which):
        return pltpu.make_async_remote_copy(
            src_ref=src_ref,
            dst_ref=dst_ref,
            send_sem=sib_s.at[which],
            recv_sem=sib_r.at[which],
            device_id={"ctx": sib},
            device_id_type=MESH,
        )

    def chip_copy(src_ref, buf, ssem, rsem, src, dest, part_at):
        span = pl.ds(part_at * piece, piece)
        return pltpu.make_async_remote_copy(
            src_ref=src_ref.at[span],
            dst_ref=buf.at[src, span],
            send_sem=ssem.at[dest, part_at],
            recv_sem=rsem.at[src, part_at],
            device_id={"ctx": 2 * dest + core},
            device_id_type=MESH,
        )

    def dkv_copy(src, dest):
        at = pl.multiple_of(dest * rows, rows)
        return pltpu.make_async_remote_copy(
            src_ref=dkv_send.at[pl.ds(at, rows)],
            dst_ref=dkv_buf.at[src],
            send_sem=dk_s.at[dest],
            recv_sem=dk_r.at[src],
            device_id={"ctx": dest},
            device_id_type=MESH,
        )

    def rs_copy(src, dest):
        at = pl.multiple_of(dest * part, part)
        return pltpu.make_async_remote_copy(
            src_ref=rs_send.at[pl.ds(at, part)],
            dst_ref=rs_buf.at[src],
            send_sem=rs_s.at[dest],
            recv_sem=rs_r.at[src],
            device_id={"grp": dest},
            device_id_type=MESH,
        )

    def ag_copy(src, dest):
        at = pl.multiple_of(src * part, part)
        return pltpu.make_async_remote_copy(
            src_ref=ag_buf.at[pl.ds(at, part)],
            dst_ref=ag_buf.at[pl.ds(at, part)],
            send_sem=ag_s.at[dest],
            recv_sem=ag_r.at[src],
            device_id={"grp": dest},
            device_id_type=MESH,
        )

    def each(low, high, action):
        def body(d, _):
            action(d)
            return 0

        lax.fori_loop(low, high, body, 0)

    decay_log = ld_ref[...]
    row_id = lax.broadcasted_iota(jnp.int32, (rows, rows), 0)
    col_id = lax.broadcasted_iota(jnp.int32, (rows, rows), 1)
    lower = row_id >= col_id
    cum = dot(lower.astype(F32), decay_log, 1, 1, HIGH)
    cum_t = dot(decay_log, (row_id <= col_id).astype(F32), 1, 0, HIGH)
    last = cum[rows - 1 :, :]
    tot_all[me] = jnp.broadcast_to(cum_t[:, rows - 1 :], tot_all.shape[1:])
    pick = (
        lax.broadcasted_iota(jnp.int32, (heads, flat), 1) // width
        == lax.broadcasted_iota(jnp.int32, (heads, flat), 0)
    ).astype(F32)
    tails = dot(jnp.exp(last - cum), pick, 1, 0, HIGH)
    heads_in = dot(jnp.exp(cum), pick, 1, 0, HIGH)
    tails_buf[...] = tails
    heads_buf[...] = heads_in
    xs_buf[...] = (tails * x_ref[...].astype(F32)).astype(BF16)
    us_buf[...] = (heads_in * su_ref[...].astype(F32)).astype(BF16)
    u_own[...] = dot(xs_buf[...], wr_ref[...], 0, 0).astype(BF16)
    t_own[...] = dot(us_buf[...], rd_ref[...], 0, 0).astype(BF16)

    kv_all[pl.ds(my_rows, rows), :HEAD_WIDTH] = kv_ref[:, 0, :]
    kv_all[pl.ds(my_rows, rows), HEAD_WIDTH:] = kv_ref[:, 1, :]

    pl.semaphore_wait(barrier, n - 1 + ng - 1)
    tot_copy(me, sib).start()

    def part_rows(base, i):
        return pl.ds(pl.multiple_of(base + i * piece, piece), piece)

    def sib_pieces(i):
        return (
            sib_copy(u_own.at[part_rows(sib_half, i)], u_sib.at[pl.ds(i * piece, piece)], 4 * i),
            sib_copy(t_own.at[part_rows(sib_half, i)], t_sib.at[pl.ds(i * piece, piece)], 4 * i + 1),
        )

    for i in range(PIECES):
        for copy in sib_pieces(i):
            copy.start()

    def send_tot(d):
        @pl.when(d // 2 != chip)
        def _():
            tot_copy(me, d).start()

    each(0, n, send_tot)

    kv_copy(me, sib).start()
    each(chip + 1, chips, lambda k: kv_copy(me, 2 * k + core).start())

    tot_copy(sib, sib).wait_recv()
    head_at = pl.multiple_of(core * half_heads, half_heads)
    first = core == 0

    def total_of(device):
        return tot_all[device, pl.ds(head_at, half_heads), :]

    grow_even = jnp.exp(total_of(2 * chip))
    grow_odd = jnp.exp(total_of(2 * chip + 1))

    def pair_of(own, other, h):
        mine = own[pl.ds(pl.multiple_of(my_half + h * width, width), width), :].astype(F32)
        theirs = other[pl.ds(h * width, width), :].astype(F32)
        return jnp.where(first, mine, theirs), jnp.where(first, theirs, mine)

    for i in range(PIECES):
        for copy in sib_pieces(i):
            copy.wait_recv()
        for h in range(i * heads_piece, (i + 1) * heads_piece):
            even, odd = pair_of(u_own, u_sib, h)
            u_chip[h * width : (h + 1) * width, :] = (
                grow_odd[h : h + 1, :] * even + odd
            ).astype(BF16)
            even, odd = pair_of(t_own, t_sib, h)
            t_chip[h * width : (h + 1) * width, :] = (
                even + grow_even[h : h + 1, :] * odd
            ).astype(BF16)
        each(chip + 1, chips, lambda d: chip_copy(u_chip, fw_buf, fw_s, fw_r, chip, d, i).start())
        each(0, chip, lambda d: chip_copy(t_chip, bw_buf, bw_s, bw_r, chip, d, i).start())

    gram = dot(rd_ref[...], wr_ref[...], 1, 1)
    gram2 = jnp.concatenate([gram, gram], axis=1)
    lane_low = lax.broadcasted_iota(jnp.int32, (rows, 2 * width), 1) < width
    mixing2 = jnp.zeros((rows, 2 * rows), F32)
    zero = jnp.zeros((rows, 2 * width), BF16)
    for p in range(heads // 2):
        cols = slice(2 * width * p, 2 * width * (p + 1))
        decays = []
        for h in (2 * p, 2 * p + 1):
            gap = cum[:, h : h + 1] - cum_t[h : h + 1, :]
            decays.append(jnp.exp(jnp.where(lower, gap, -jnp.inf)))
        decay = jnp.concatenate(decays, axis=1)
        weights = (decay * gram2).astype(BF16)
        x_pair = x_ref[:, cols]
        x_split = jnp.concatenate(
            [jnp.where(lane_low, x_pair, zero), jnp.where(lane_low, zero, x_pair)], axis=0
        )
        su_pair = su_ref[:, cols]
        mixing2 = mixing2 + decay * dot(su_pair, x_split, 1, 1)
        outt = dot(weights, x_split, 1, 0)
        so_ref[:, cols] = outt.astype(BF16)
        back = dot(weights, su_pair, 0, 0)
        ig_ref[:, cols] = jnp.where(lane_low, back[:rows], back[rows:]).astype(BF16)
    mixing = (mixing2[:, :rows] + mixing2[:, rows:]).astype(BF16)
    n_state = wr_ref.shape[1]
    rw_acc[:, :n_state] = dot(mixing, rd_ref[...], 0, 0)
    rw_acc[:, n_state:] = dot(mixing, wr_ref[...], 1, 0)

    block = 2 * rows
    key_id = lax.broadcasted_iota(jnp.int32, (block, rows), 0)
    query_id = lax.broadcasted_iota(jnp.int32, (block, rows), 1)

    def relay(k):
        kv_copy(2 * k + core, me).wait_recv()
        kv_copy(2 * k + core, sib, 2 * k).start()

    each(0, chip, relay)

    top_buf[...] = jnp.full(top_buf.shape, -jnp.inf, F32)
    norm_buf[...] = jnp.zeros(norm_buf.shape, F32)
    outt_buf[...] = jnp.zeros(outt_buf.shape, F32)

    def forward(j):
        kv_copy(2 * j + 1 - core, sib).wait_recv()
        at = pl.multiple_of(j * block, block)
        keys = kv_all[pl.ds(at, block), :HEAD_WIDTH]
        values_t = kv_all[pl.ds(at, block), HEAD_WIDTH:].T
        valid = key_id + j * block <= query_id + me * rows
        for h in range(heads_q):
            q = q_ref[:, h * HEAD_WIDTH : (h + 1) * HEAD_WIDTH]
            scores = jnp.where(valid, dot(keys, q, 1, 1) * scale, -jnp.inf)
            top = top_buf[h : h + 1, :]
            new_top = jnp.maximum(top, jnp.max(scores, axis=0, keepdims=True))
            shrink = jnp.exp(top - new_top)
            probs = jnp.exp(scores - new_top)
            norm_buf[h : h + 1, :] = norm_buf[h : h + 1, :] * shrink + jnp.sum(
                probs, axis=0, keepdims=True
            )
            top_buf[h : h + 1, :] = new_top
            outt_buf[h] = outt_buf[h] * shrink + dot(values_t, probs.astype(BF16), 1, 0)

    each(0, chip + 1, forward)

    for h in range(heads_q):
        cols = slice(h * HEAD_WIDTH, (h + 1) * HEAD_WIDTH)
        norm = norm_buf[h : h + 1, :]
        low = (outt_buf[h] / norm).astype(BF16).astype(F32)
        out = low.T
        out_ref[:, cols] = out.astype(BF16)
        up_t = up_ref[:, cols].astype(F32).T
        dots_buf[h : h + 1, :] = jnp.sum(up_t * low, axis=0, keepdims=True)
        top_buf[h : h + 1, :] = top_buf[h : h + 1, :] + jnp.log(norm)
    dqt_buf[...] = jnp.zeros(dqt_buf.shape, F32)

    def backward(j):
        at = pl.multiple_of(j * block, block)
        keys = kv_all[pl.ds(at, block), :HEAD_WIDTH]
        values = kv_all[pl.ds(at, block), HEAD_WIDTH:]
        keys_t = keys.T
        valid = key_id + j * block <= query_id + me * rows
        key_acc = jnp.zeros((block, HEAD_WIDTH), F32)
        value_acc = jnp.zeros((block, HEAD_WIDTH), F32)
        for h in range(heads_q):
            cols = slice(h * HEAD_WIDTH, (h + 1) * HEAD_WIDTH)
            q = q_ref[:, cols]
            up = up_ref[:, cols]
            scores = jnp.where(valid, dot(keys, q, 1, 1) * scale, -jnp.inf)
            exact = jnp.exp(scores - top_buf[h : h + 1, :])
            probs_grad = dot(values, up, 1, 1)
            scores_grad = (exact * (probs_grad - dots_buf[h : h + 1, :]) * scale).astype(BF16)
            dqt_buf[h] = dqt_buf[h] + dot(keys_t, scores_grad, 1, 0)
            key_acc = key_acc + dot(scores_grad, q, 1, 0)
            value_acc = value_acc + dot(exact.astype(BF16), up, 1, 0)
        dkv_send[pl.ds(at, block), :HEAD_WIDTH] = key_acc.astype(BF16)
        dkv_send[pl.ds(at, block), HEAD_WIDTH:] = value_acc.astype(BF16)

        @pl.when(j == chip)
        def _():
            own = core == 0
            dkv_own[:, :HEAD_WIDTH] = jnp.where(own, key_acc[:rows], key_acc[rows:])
            dkv_own[:, HEAD_WIDTH:] = jnp.where(own, value_acc[:rows], value_acc[rows:])

    each(0, chip + 1, backward)

    s_acc[...] = jnp.zeros(s_acc.shape, F32)
    a_acc[...] = jnp.zeros(a_acc.shape, F32)

    def wait_tot(d):
        @pl.when(d // 2 != chip)
        def _():
            tot_copy(d, sib).wait_recv()

    each(0, n, wait_tot)

    def fold(acc, buf, rsem, src_ref, i, k):
        chip_copy(src_ref, buf, rsem, rsem, k, chip, i).wait_recv()
        grow = jnp.exp(total_of(2 * k) + total_of(2 * k + 1))
        for h in range(i * heads_piece, (i + 1) * heads_piece):
            at = slice(h * width, (h + 1) * width)
            acc[at, :] = grow[h : h + 1, :] * acc[at, :] + buf[k, at, :].astype(F32)

    def back_pieces(i, base):
        span = pl.ds(i * piece, piece)
        return (
            sib_copy(s_send.at[span], s_full.at[part_rows(base, i)], 4 * i + 2),
            sib_copy(a_send.at[span], a_full.at[part_rows(base, i)], 4 * i + 3),
        )

    def add_states(i):
        for copy in back_pieces(i, sib_half):
            copy.wait_recv()
        for at in (i * piece, half + i * piece):
            span = slice(at, at + piece)
            rw_acc[:, n_state:] = rw_acc[:, n_state:] + dot(us_buf[:, span], s_full[span, :], 1, 0)
            rw_acc[:, :n_state] = rw_acc[:, :n_state] + dot(xs_buf[:, span], a_full[span, :], 1, 0)

    for i in range(PIECES):
        each(0, chip, lambda k: fold(s_acc, fw_buf, fw_r, u_chip, i, k))
        each(
            0,
            chips - 1 - chip,
            lambda k: fold(a_acc, bw_buf, bw_r, t_chip, i, chips - 1 - k),
        )
        for h in range(i * heads_piece, (i + 1) * heads_piece):
            at = slice(h * width, (h + 1) * width)
            mine_at = pl.ds(pl.multiple_of(my_half + h * width, width), width)
            even_u, _ = pair_of(u_own, u_sib, h)
            state_even = s_acc[at, :]
            state_odd = grow_even[h : h + 1, :] * state_even + even_u
            s_full[mine_at, :] = jnp.where(first, state_even, state_odd).astype(BF16)
            s_send[at, :] = jnp.where(first, state_odd, state_even).astype(BF16)
            _, odd_t = pair_of(t_own, t_sib, h)
            adj_odd = a_acc[at, :]
            adj_even = grow_odd[h : h + 1, :] * adj_odd + odd_t
            a_full[mine_at, :] = jnp.where(first, adj_even, adj_odd).astype(BF16)
            a_send[at, :] = jnp.where(first, adj_odd, adj_even).astype(BF16)
        for copy in back_pieces(i, my_half):
            copy.start()
        if i > 0:
            add_states(i - 1)
    add_states(PIECES - 1)

    rs_send[...] = rw_acc[...].astype(BF16)

    def send_rs(d):
        @pl.when(d != grp)
        def _():
            rs_copy(grp, d).start()

    each(0, ng, send_rs)
    each(0, me, lambda d: dkv_copy(me, d).start())
    so_ref[...] = (
        so_ref[...].astype(F32) + heads_buf[...] * dot(rd_ref[...], s_full[...], 1, 1)
    ).astype(BF16)
    ig_ref[...] = (
        ig_ref[...].astype(F32) + tails_buf[...] * dot(wr_ref[...], a_full[...], 1, 1)
    ).astype(BF16)

    total = rw_acc[pl.ds(pl.multiple_of(grp * part, part), part), :]
    rw_acc[pl.ds(0, part), :] = total

    def take_rs(d):
        @pl.when(d != grp)
        def _():
            rs_copy(d, d).wait_recv()
            rw_acc[pl.ds(0, part), :] = rw_acc[pl.ds(0, part), :] + rs_buf[d].astype(F32)

    each(0, ng, take_rs)
    ag_buf[pl.ds(pl.multiple_of(grp * part, part), part), :] = rw_acc[pl.ds(0, part), :].astype(
        BF16
    )

    def send_ag(d):
        @pl.when(d != grp)
        def _():
            ag_copy(grp, d).start()

    each(0, ng, send_ag)

    for h in range(heads_q):
        qg_ref[:, h * HEAD_WIDTH : (h + 1) * HEAD_WIDTH] = dqt_buf[h].T.astype(BF16)

    def take_dkv(d):
        dkv_copy(d, me).wait_recv()
        dkv_own[...] = dkv_own[...] + dkv_buf[d].astype(F32)

    each(me + 1, n, take_dkv)
    kvg_ref[...] = dkv_own[...].astype(BF16)

    def take_ag(d):
        @pl.when(d != grp)
        def _():
            ag_copy(d, d).wait_recv()

    each(0, ng, take_ag)
    wg_ref[...] = ag_buf[:, :n_state]
    rg_ref[...] = ag_buf[:, n_state:]

    def end_ctx(d):
        @pl.when(d != me)
        def _():
            tot_copy(me, d).wait_send()

            @pl.when(d < me)
            def _():
                dkv_copy(me, d).wait_send()

    each(0, n, end_ctx)
    kv_copy(me, sib).wait_send()
    each(chip + 1, chips, lambda k: kv_copy(me, 2 * k + core).wait_send())
    each(0, chip, lambda k: kv_copy(2 * k + core, sib, 2 * k).wait_send())
    for i in range(PIECES):
        for copy in sib_pieces(i) + back_pieces(i, my_half):
            copy.wait_send()
        each(
            chip + 1,
            chips,
            lambda d: chip_copy(u_chip, fw_buf, fw_s, fw_r, chip, d, i).wait_send(),
        )
        each(0, chip, lambda d: chip_copy(t_chip, bw_buf, bw_s, bw_r, chip, d, i).wait_send())

    def end_grp(d):
        @pl.when(d != grp)
        def _():
            rs_copy(grp, d).wait_send()
            ag_copy(grp, d).wait_send()

    each(0, ng, end_grp)


def store(*refs):
    for index in range(7):
        source, target = refs[index], refs[7 + index]
        if index == 2:
            target[:, 0, :] = source[:, :HEAD_WIDTH]
            target[:, 1, :] = source[:, HEAD_WIDTH:]
        else:
            target[...] = source[...]


def on_device(
    queries,
    key_value_pair,
    attention_upstream,
    ssm_input,
    write_vec,
    read_vec,
    log_decay,
    ssm_upstream,
):
    n = lax.axis_size("ctx")
    ng = lax.axis_size("grp")
    rows, cols = queries.shape
    heads_q = cols // HEAD_WIDTH
    flat = ssm_input.shape[1]
    heads = log_decay.shape[1]
    n_state = write_vec.shape[1]
    chips = n // 2
    half = flat // 2
    vm = pltpu.VMEM
    dma = pltpu.SemaphoreType.DMA
    outs = pl.pallas_call(
        functools.partial(kernel, n, ng),
        out_shape=(
            jax.ShapeDtypeStruct((rows, cols), BF16),
            jax.ShapeDtypeStruct((rows, cols), BF16),
            jax.ShapeDtypeStruct((rows, 2 * HEAD_WIDTH), BF16),
            jax.ShapeDtypeStruct((rows, flat), BF16),
            jax.ShapeDtypeStruct((rows, flat), BF16),
            jax.ShapeDtypeStruct((rows, n_state), BF16),
            jax.ShapeDtypeStruct((rows, n_state), BF16),
        ),
        in_specs=[pl.BlockSpec(memory_space=pltpu.VMEM)] * 8,
        out_specs=[pl.BlockSpec(memory_space=pltpu.VMEM)] * 7,
        scratch_shapes=[
            vm((n * rows, 2 * HEAD_WIDTH), BF16),
            vm((n, heads, n_state), F32),
            vm((flat, n_state), BF16),
            vm((flat, n_state), BF16),
            vm((half, n_state), BF16),
            vm((half, n_state), BF16),
            vm((half, n_state), BF16),
            vm((half, n_state), BF16),
            vm((chips, half, n_state), BF16),
            vm((chips, half, n_state), BF16),
            vm((half, n_state), F32),
            vm((half, n_state), F32),
            vm((half, n_state), BF16),
            vm((half, n_state), BF16),
            vm((flat, n_state), BF16),
            vm((flat, n_state), BF16),
            vm((rows, flat), BF16),
            vm((rows, flat), BF16),
            vm((rows, flat), F32),
            vm((rows, flat), F32),
            vm((rows, 2 * n_state), F32),
            vm((rows, 2 * n_state), BF16),
            vm((ng, rows // ng, 2 * n_state), BF16),
            vm((rows, 2 * n_state), BF16),
            vm((heads_q, rows), F32),
            vm((heads_q, rows), F32),
            vm((heads_q, rows), F32),
            vm((heads_q, HEAD_WIDTH, rows), F32),
            vm((heads_q, HEAD_WIDTH, rows), F32),
            vm((n * rows, 2 * HEAD_WIDTH), BF16),
            vm((n, rows, 2 * HEAD_WIDTH), BF16),
            vm((rows, 2 * HEAD_WIDTH), F32),
            dma((n,)),
            dma((n,)),
            dma((n,)),
            dma((n,)),
            dma((4 * PIECES,)),
            dma((4 * PIECES,)),
            dma((chips, PIECES)),
            dma((chips, PIECES)),
            dma((chips, PIECES)),
            dma((chips, PIECES)),
            dma((n,)),
            dma((n,)),
            dma((ng,)),
            dma((ng,)),
            dma((ng,)),
            dma((ng,)),
        ],
        compiler_params=pltpu.CompilerParams(
            collective_id=0, has_side_effects=True, vmem_limit_bytes=56 * 1024 * 1024
        ),
    )(
        queries,
        key_value_pair,
        attention_upstream,
        ssm_input,
        write_vec,
        read_vec,
        log_decay.T,
        ssm_upstream,
    )
    return pl.pallas_call(
        store,
        out_shape=(
            jax.ShapeDtypeStruct((rows, cols), BF16),
            jax.ShapeDtypeStruct((rows, cols), BF16),
            jax.ShapeDtypeStruct((rows, 2, HEAD_WIDTH), BF16),
            jax.ShapeDtypeStruct((rows, flat), BF16),
            jax.ShapeDtypeStruct((rows, flat), BF16),
            jax.ShapeDtypeStruct((rows, n_state), BF16),
            jax.ShapeDtypeStruct((rows, n_state), BF16),
        ),
        in_specs=[pl.BlockSpec(memory_space=pltpu.VMEM)] * 7,
        out_specs=[pl.BlockSpec(memory_space=pltpu.VMEM)] * 7,
    )(*outs)


def solution(mesh):
    return jax.shard_map(
        on_device,
        mesh=mesh,
        in_specs=(
            P("ctx", "grp"),
            P("ctx", None, "grp"),
            P("ctx", "grp"),
            P("ctx", "grp"),
            P("ctx", None),
            P("ctx", None),
            P("ctx", "grp"),
            P("ctx", "grp"),
        ),
        out_specs=(
            P("ctx", "grp"),
            P("ctx", "grp"),
            P("ctx", None, "grp"),
            P("ctx", "grp"),
            P("ctx", "grp"),
            P("ctx", None),
            P("ctx", None),
        ),
        check_vma=False,
    )
```
